1024 devices in a mesh: dom: 64 (over y, x), grp: 16 (over z, core).
Axes of the slice: x: 8, y: 8, z: 8, core: 2. Of those that a mesh axis runs over, the one named last changes fastest.
Arguments:
- history: bfloat16 [128, 4, 128, 4096], P('dom', None, 'grp'), may hold values from -6 to 6
- face_patch: int32 [128, 6], replicated, may hold values from -1 to 127, as said below
- refined: int32 [128], replicated, may hold values 0 or 1
- dest_slot: int32 [128], replicated, may hold values from 0 to 127, as said below
- w_in: bfloat16 [640, 512], replicated, may hold values from -0.25 to 0.25
- in_bias: float32 [512], replicated, may hold values from -3 to 3
- w_out: bfloat16 [512, 128], replicated, may hold values from -0.25 to 0.25
Outputs:
- new_states: bfloat16 [128, 2, 128, 4096], P('dom', None, 'grp')
The draws below stay inside these ranges and needn't reach their ends.
Inputs may be any that keep to these rules, and one draw needn't show every extreme that they name: `dest_slot`: A permutation of the slots. Slot s lies on dom index s // 2; patch p starts at slot p, on index p // 2. No patch moves by more than one index of dom, from one index at most 1 patches go to each neighbouring index, and 1 is reached between some pair of indices. `face_patch`: -1 where the face lies on the window's boundary, else a patch other than p, aligned with p cell for cell on that face; its dom index is within one of p's both before and after rebalancing.
All inputs are finite; a program needn't handle non-finite values.
Results may differ from the reference program's by a relative error of at most 0.0071.
Values may be sent and summed in bfloat16 or wider, within the bound.
A program may use at most 128 MiB of HBM per device.

```python
import jax
import jax.numpy as jnp
import numpy as np
from jax import lax

CH = 128
HID = 512
SIDE = 16
HIST = 4
PD = 2
MOVE = 1
PATCHES = 128


def migration_plan(key):
    dom_count = PATCHES // PD
    key_counts, key_pick, key_order = jax.random.split(jax.random.fold_in(key, 7), 3)
    swap_counts = jax.random.randint(key_counts, (dom_count - 1,), 0, MOVE + 1)
    forced = jax.random.randint(key_pick, (), 0, dom_count - 1)
    swap_counts = jnp.where(jnp.arange(dom_count - 1) == forced, MOVE, swap_counts)
    orders = jax.vmap(lambda sub_key: jax.random.permutation(sub_key, PD))(jax.random.split(key_order, dom_count))
    bounds = jnp.arange(dom_count - 1)
    right_ids = bounds[:, None] * PD + orders[:-1, MOVE:2 * MOVE]
    left_ids = (bounds[:, None] + 1) * PD + orders[1:, :MOVE]
    active = jnp.arange(MOVE)[None, :] < swap_counts[:, None]
    dest_ids = jnp.arange(PATCHES, dtype=jnp.int32)
    dest_ids = dest_ids.at[right_ids.reshape(-1)].set(jnp.where(active, left_ids, right_ids).reshape(-1))
    dest_ids = dest_ids.at[left_ids.reshape(-1)].set(jnp.where(active, right_ids, left_ids).reshape(-1))
    return dest_ids.astype(jnp.int32)


def draw_dest_slot(key, part):
    return migration_plan(key)


def draw_face_patch(key, part):
    dest_ids = migration_plan(key)
    key_pick, key_edge = jax.random.split(jax.random.fold_in(key, 19))
    patch_ids = jnp.arange(PATCHES, dtype=jnp.int32)[:, None]
    home_dev = patch_ids // PD
    low_end = jnp.maximum(home_dev - 1, 0) * PD
    high_end = jnp.minimum(home_dev + 2, PATCHES // PD) * PD
    raw_pick = jax.random.randint(key_pick, (PATCHES, 6), 0, 3 * PD)
    partner = low_end + raw_pick % (high_end - low_end)
    too_far = jnp.abs(dest_ids[partner] // PD - dest_ids[patch_ids] // PD) > 1
    on_edge = jax.random.randint(key_edge, (PATCHES, 6), 0, 6) == 0
    return jnp.where(too_far | on_edge | (partner == patch_ids), -1, partner).astype(jnp.int32)


def set_ends(values, rng, low, top_value):
    longest = values.shape.index(max(values.shape))
    spots = []
    for shift in (0, 1):
        where = [jax.random.randint(jax.random.fold_in(rng, axis), (), 0, length) for axis, length in enumerate(values.shape)]
        where[longest] = (where[longest] + shift) % values.shape[longest]
        spots.append(tuple(where))
    return values.at[spots[0]].set(low).at[spots[1]].set(top_value)


def shard_levels(stream_key, extent, shards, low, high):
    level, own = 1.0, jax.random.fold_in(stream_key, 6)
    for dim, shards_of in shards:
        draws = jnp.exp(jax.random.uniform(jax.random.fold_in(own, dim), (shards_of,), jnp.float32, low / len(shards), high / len(shards)))
        level = level * jnp.repeat(draws, extent[dim] // shards_of).reshape([-1 if axis == dim else 1 for axis in range(len(extent))])
    return level


def noise(own_key, extent, scale, bound, cuts=(), kind=jnp.bfloat16):
    result = jax.random.normal(own_key, extent, jnp.float32) * scale
    if len(cuts) > 0:
        result = shard_levels(own_key, extent, cuts, -0.22, 0.18) * result
    return jnp.clip(result, min=-bound, max=bound).astype(kind)


def setup_inputs(seed: int = 0) -> dict:
    splits = jax.random.split(jax.random.key(seed), 8)
    history = noise(splits[0], (PATCHES, HIST, CH, SIDE**3), 1.0, 6.0, ((0, 64), (2, 16)))
    face_patch = draw_face_patch(jax.random.fold_in(splits[7], 71), 0)
    refined = set_ends((jax.random.randint(splits[2], (PATCHES,), 0, 4) < 1).astype(jnp.int32), jax.random.fold_in(splits[2], 1), 0, 1)
    dest_slot = draw_dest_slot(jax.random.fold_in(splits[7], 71), 0)
    w_in = noise(splits[4], ((HIST + 1) * CH, HID), ((HIST + 1) * CH) ** -0.5, 0.25)
    in_bias = noise(splits[5], (HID,), 0.5, 3.0, (), jnp.float32)
    w_out = noise(splits[6], (HID, CH), HID ** -0.5, 0.25)
    return dict(history=history, face_patch=face_patch, refined=refined, dest_slot=dest_slot, w_in=w_in, in_bias=in_bias, w_out=w_out)


OPPOSITE = np.array([1, 0, 3, 2, 5, 4])


def face_layers(grid_field):
    return jnp.stack([grid_field[..., 0, :, :], grid_field[..., -1, :, :],
                      grid_field[..., :, 0, :], grid_field[..., :, -1, :],
                      grid_field[..., :, :, 0], grid_field[..., :, :, -1]], axis=-4)


def surround(grid_field, picked):
    widths = [(0, 0)] * (grid_field.ndim - 3) + [(1, 1)] * 3
    padded = jnp.pad(grid_field, widths)
    padded = padded.at[..., 0, 1:-1, 1:-1].set(picked[..., 0, :, :, :])
    padded = padded.at[..., -1, 1:-1, 1:-1].set(picked[..., 1, :, :, :])
    padded = padded.at[..., 1:-1, 0, 1:-1].set(picked[..., 2, :, :, :])
    padded = padded.at[..., 1:-1, -1, 1:-1].set(picked[..., 3, :, :, :])
    padded = padded.at[..., 1:-1, 1:-1, 0].set(picked[..., 4, :, :, :])
    padded = padded.at[..., 1:-1, 1:-1, -1].set(picked[..., 5, :, :, :])
    neighbour_sum = (padded[..., 2:, 1:-1, 1:-1] + padded[..., :-2, 1:-1, 1:-1]
                     + padded[..., 1:-1, 2:, 1:-1] + padded[..., 1:-1, :-2, 1:-1]
                     + padded[..., 1:-1, 1:-1, 2:] + padded[..., 1:-1, 1:-1, :-2])
    return neighbour_sum - 6.0 * grid_field


def advance(history, face_patch, refined, w_in, in_bias, w_out):
    how_many = history.shape[0]
    newest = history[:, 0].astype(jnp.float32).reshape(how_many, CH, SIDE, SIDE, SIDE)
    layers = face_layers(newest)[:, OPPOSITE]
    usable = face_patch >= 0
    picked = layers[jnp.maximum(face_patch, 0), jnp.arange(6)[None, :]]
    picked = jnp.where(usable[:, :, None, None, None], picked, jnp.zeros_like(picked))
    step_sizes = 1.0 - 0.5 * refined.astype(jnp.float32)

    def one_patch(patch_args):
        patch_states, faces, step_size = patch_args
        grid_field = patch_states[0].astype(jnp.float32).reshape(CH, SIDE, SIDE, SIDE)
        spread = surround(grid_field, faces).reshape(CH, SIDE ** 3).astype(jnp.bfloat16)
        inputs = jnp.concatenate([patch_states, spread[None]], 0).reshape((HIST + 1) * CH, SIDE ** 3)
        preact = jnp.dot(inputs.T, w_in, preferred_element_type=jnp.float32) + in_bias
        hidden = jax.nn.silu(preact).astype(jnp.bfloat16)
        update = jnp.dot(hidden, w_out, preferred_element_type=jnp.float32).astype(jnp.bfloat16)
        return (patch_states[0].astype(jnp.float32) + step_size * update.T.astype(jnp.float32)).astype(jnp.bfloat16)

    return lax.map(one_patch, (history, picked, step_sizes))


def reference(history, face_patch, refined, dest_slot, w_in, in_bias, w_out):
    first_state = advance(history, face_patch, refined, w_in, in_bias, w_out)
    carried = jnp.concatenate([first_state[:, None], history[:, :HIST - 1]], 1)
    second_state = advance(carried, face_patch, refined, w_in, in_bias, w_out)
    both_states = jnp.stack([first_state, second_state], 1)
    return jnp.zeros_like(both_states).at[dest_slot].set(both_states)
```

```python
import functools

import jax
import jax.numpy as jnp
from jax import lax
from jax.experimental import pallas as pl
from jax.experimental.pallas import tpu as pltpu
from jax.sharding import PartitionSpec as P

MESH = pl.DeviceIdType.MESH
F32, BF16 = jnp.float32, jnp.bfloat16


def surrogate(sizes, dest, face, refined, hist, w_in, w_out, bias, out, own, stage, moved, mine, cells, state1, state2,
              xm1, xp1, xm2, xp2, edge1, edge2, w_raw, wo_raw, wt, wot, bcol, feed, base, adj, pick, place,
              load_sem, mig_send, mig_recv, go_send, go_recv, back_send, back_recv, halo_send, halo_recv):
    doms, grps, side, hist_len, ch, hid = sizes
    plane = side * side
    block = ch // grps
    d, g = lax.axis_index("dom"), lax.axis_index("grp")
    left, right = lax.rem(d + doms - 1, doms), lax.rem(d + 1, doms)
    up, down = lax.rem(g + 1, grps), lax.rem(g + grps - 1, grps)
    my_plane = down

    def wait_for(ref, sem):
        pltpu.make_async_copy(ref, ref, sem).wait()

    loads = [pltpu.make_async_copy(hist.at[:, k], own.at[k], load_sem.at[k]) for k in range(hist_len)]
    loads.append(pltpu.make_async_copy(w_in, w_raw, load_sem.at[hist_len]))
    loads.append(pltpu.make_async_copy(w_out, wo_raw, load_sem.at[hist_len + 1]))
    for load in loads:
        load.start()

    barrier = pltpu.get_barrier_semaphore()

    def greet(i, carry):
        pl.semaphore_signal(barrier, inc=1, device_id=(d, lax.rem(g + i, grps)), device_id_type=MESH)
        return carry

    lax.fori_loop(1, grps, greet, 0)
    for beside in (left, right):
        pl.semaphore_signal(barrier, inc=1, device_id=(beside, g), device_id_type=MESH)

    @pl.when(g < 2)
    def _():
        for beside in (left, right):
            pl.semaphore_signal(barrier, inc=1, device_id=(beside, 1 - g), device_id_type=MESH)

    patches = 2 * doms
    cands = [lax.rem(2 * d + patches - 2 + i, patches) for i in range(6)]
    goals = [dest[c] for c in cands]
    go_left = jnp.where(goals[3] // 2 == d - 1, 1, 0)
    go_right = jnp.where(goals[3] // 2 == d + 1, 1, 0)
    origin, beside_slot, step_size = [], [], []
    for j in range(2):
        place_of = jnp.int32(0)
        owner = jnp.int32(0)
        for i in range(6):
            hit = goals[i] == 2 * d + j
            place_of = jnp.where(hit, i, place_of)
            owner = jnp.where(hit, cands[i], owner)
        origin.append(place_of)
        row = []
        for f in range(6):
            q = face[f, owner]
            pos = jnp.clip(dest[jnp.maximum(q, 0)] - 2 * (d - 1), 0, 5)
            row.append(jnp.where(q >= 0, pos, 6))
        beside_slot.append(row)
        step_size.append(1.0 - 0.5 * refined[owner].astype(F32))

    for buf in (xm1, xp1, xm2, xp2):
        buf[6] = jnp.zeros(buf.shape[1:], BF16)

    for k in range(hist_len):
        loads[k].wait()
    pl.semaphore_wait(barrier, jnp.where(g < 2, grps + 3, grps + 1))

    moves = []
    for k in range(hist_len):
        for side_of, (which, target) in enumerate(((go_right, right), (go_left, left))):
            stage[k, side_of] = jnp.where(which == 1, own[k, 1], own[k, 0])
            move = pltpu.make_async_remote_copy(
                src_ref=stage.at[k, side_of], dst_ref=moved.at[k, side_of], send_sem=mig_send.at[k, side_of],
                recv_sem=mig_recv.at[k, side_of], device_id=(target, g), device_id_type=MESH)
            move.start()
            moves.append(move)

    def lanes_of(device):
        return pl.ds(pl.multiple_of(lax.rem(device + grps - 1, grps) * plane, plane), plane)

    for k in range(hist_len):
        moves[2 * k].wait_recv()
        moves[2 * k + 1].wait_recv()
        for j in range(2):
            at = origin[j]
            stays = jnp.where(at == 2, own[k, 0], own[k, 1])
            comes = jnp.where(at < 2, moved[k, 0], moved[k, 1])
            mine[k, j] = jnp.where((at == 2) | (at == 3), stays, comes)

        def send(i, carry, k=k):
            peer = lax.rem(g + i, grps)
            pltpu.make_async_remote_copy(
                src_ref=mine.at[k, :, :, lanes_of(peer)], dst_ref=cells.at[k, :, g], send_sem=go_send.at[k],
                recv_sem=go_recv.at[k], device_id=(d, peer), device_id_type=MESH).start()
            return carry

        lax.fori_loop(1, grps, send, 0)
        pltpu.make_async_copy(mine.at[k, :, :, lanes_of(g)], cells.at[k, :, g], go_recv.at[k]).start()

    r = lax.broadcasted_iota(jnp.int32, (plane, plane), 0)
    c = lax.broadcasted_iota(jnp.int32, (plane, plane), 1)
    ry, rz, cy, cz = r // side, r % side, c // side, c % side
    beside_cell = ((ry == cy) & (jnp.abs(rz - cz) == 1)) | ((rz == cz) & (jnp.abs(ry - cy) == 1))
    adj[...] = jnp.where(r == c, -6.0, jnp.where(beside_cell, 1.0, 0.0)).astype(BF16)
    width = 8 * side

    def layer_cell(layer, k):
        along_y = jnp.where(layer == 0, k, plane - side + k)
        along_z = jnp.where(layer == 2, k * side, k * side + side - 1)
        return jnp.where(layer < 2, along_y, along_z)

    r = lax.broadcasted_iota(jnp.int32, (plane, width), 0)
    c = lax.broadcasted_iota(jnp.int32, (plane, width), 1)
    for j in range(2):
        hit = (r == layer_cell((c // side) % 4, c % side)) & (c // (4 * side) == j)
        pick[j] = jnp.where(hit, 1.0, 0.0).astype(BF16)
    r = lax.broadcasted_iota(jnp.int32, (width, plane), 0)
    c = lax.broadcasted_iota(jnp.int32, (width, plane), 1)
    layer = (r // side) % 4
    opposite = jnp.where(layer % 2 == 0, layer + 1, layer - 1)
    place[...] = jnp.where(c == layer_cell(opposite, r % side), 1.0, 0.0).astype(BF16)
    bcol[...] = jnp.broadcast_to(bias[...], (bcol.shape[1], hid)).T
    loads[hist_len].wait()
    loads[hist_len + 1].wait()
    for k in range(hist_len + 1):
        wt[:, k * ch:(k + 1) * ch] = w_raw[k * ch:(k + 1) * ch, :].astype(F32).T.astype(BF16)
    wot[...] = wo_raw[...].astype(F32).T.astype(BF16)

    lane = lax.broadcasted_iota(jnp.int32, (ch, width), 1)
    lane_layer, lane_patch = (lane // side) % 4, lane // (4 * side)

    def wide(ref_value):
        return ref_value.astype(F32).reshape(ch, plane)

    def start_halo(t, state, xm, xp, edge):
        rows = [wide(state[j]).astype(BF16) for j in range(2)]
        edges = sum(jnp.dot(rows[j], pick[j], preferred_element_type=F32) for j in range(2))
        edge[1] = edges.astype(BF16)
        plans = [(state, xm.at[pl.ds(2, 2)], (d, up)), (state, xp.at[pl.ds(2, 2)], (d, down)),
                 (edge.at[1], edge.at[0], (right, g)), (edge.at[1], edge.at[2], (left, g))]
        copies = [pltpu.make_async_remote_copy(
            src_ref=src, dst_ref=dst, send_sem=halo_send.at[t, i], recv_sem=halo_recv.at[t, i], device_id=to,
            device_id_type=MESH) for i, (src, dst, to) in enumerate(plans)]

        def over_the_rim(buf):
            return [pltpu.make_async_remote_copy(
                src_ref=state, dst_ref=buf.at[pl.ds(at, 2)], send_sem=halo_send.at[t, 4 + i],
                recv_sem=halo_recv.at[t, 4 + i], device_id=(to, 1 - g), device_id_type=MESH)
                for i, (at, to) in enumerate(((0, right), (4, left)))]

        @pl.when(g == 0)
        def _():
            for copy in over_the_rim(xm):
                copy.start()

        @pl.when(g == 1)
        def _():
            for copy in over_the_rim(xp):
                copy.start()

        for copy in copies:
            copy.start()

        def finish():
            for copy in copies:
                copy.wait()

            @pl.when(g == 0)
            def _():
                for copy in over_the_rim(xp):
                    copy.wait()

            @pl.when(g == 1)
            def _():
                for copy in over_the_rim(xm):
                    copy.wait()

        return finish

    def laplace(state, xm, xp, edge, j):
        near = jnp.dot(wide(state[j]).astype(BF16), adj[...], preferred_element_type=F32)
        slots = beside_slot[j]
        wanted = jnp.where(lane_layer == 0, slots[3], jnp.where(lane_layer == 1, slots[2], jnp.where(
            lane_layer == 2, slots[5], slots[4])))
        faces = jnp.zeros((ch, width), F32)
        for i in range(3):
            faces = jnp.where(wanted == 2 * i + lane_patch, edge[i].astype(F32), faces)
        near = near + jnp.dot(faces.astype(BF16), place[...], preferred_element_type=F32)
        before = xm[jnp.where(my_plane == 0, slots[0], 2 + j)]
        after = xp[jnp.where(my_plane == grps - 1, slots[1], 2 + j)]
        return (near + wide(before) + wide(after)).astype(BF16)

    def beside_bias(value):
        return value + jnp.concatenate([bcol[...]] * (plane // bcol.shape[1]), 1)

    def next_state(pre, start, j):
        hidden = (pre / (1.0 + jnp.exp(-pre))).astype(BF16)
        update = jnp.dot(wot[...], hidden, preferred_element_type=F32).astype(BF16)
        fresh = start + step_size[j] * update.astype(F32)
        return fresh.reshape(grps, block, plane).astype(BF16)

    def send_back(t, state):
        def send(i, carry):
            peer = lax.rem(g + i, grps)
            pltpu.make_async_remote_copy(
                src_ref=state.at[:, peer], dst_ref=out.at[:, t, :, lanes_of(g)], send_sem=back_send.at[t],
                recv_sem=back_recv.at[t], device_id=(d, peer), device_id_type=MESH).start()
            return carry

        lax.fori_loop(1, grps, send, 0)
        pltpu.make_async_copy(state.at[:, g], out.at[:, t, :, lanes_of(g)], back_recv.at[t]).start()

    newest = cells.at[0]
    wait_for(newest, go_recv.at[0])
    finish1 = start_halo(0, newest, xm1, xp1, edge1)
    for k in range(hist_len):
        if k > 0:
            wait_for(cells.at[k], go_recv.at[k])
        for j in range(2):
            feed[k * ch:(k + 1) * ch, j * plane:(j + 1) * plane] = wide(cells[k, j]).astype(BF16)
    finish1()
    for j in range(2):
        cols = slice(j * plane, (j + 1) * plane)
        feed[hist_len * ch:, cols] = laplace(newest, xm1, xp1, edge1, j)
        pre = beside_bias(jnp.dot(wt[...], feed[:, cols], preferred_element_type=F32))
        state1[j] = next_state(pre, wide(newest[j]), j)

    finish2 = start_halo(1, state1, xm2, xp2, edge2)
    send_back(0, state1)
    for j in range(2):
        cols = slice(j * plane, (j + 1) * plane)
        kept = jnp.dot(wt[:, ch:hist_len * ch], feed[:(hist_len - 1) * ch, cols], preferred_element_type=F32)
        fresh = jnp.dot(wt[:, :ch], wide(state1[j]).astype(BF16), preferred_element_type=F32)
        base[:, cols] = beside_bias(kept + fresh)
    finish2()
    for j in range(2):
        cols = slice(j * plane, (j + 1) * plane)
        spread = laplace(state1, xm2, xp2, edge2, j)
        pre = base[:, cols] + jnp.dot(wt[:, hist_len * ch:], spread, preferred_element_type=F32)
        state2[j] = next_state(pre, wide(state1[j]), j)
    send_back(1, state2)

    for move in moves:
        move.wait_send()
    for k in range(hist_len):
        wait_for(cells.at[k, :, pl.ds(0, grps - 1)], go_send.at[k])
    for t in range(2):
        wait_for(state1.at[:, pl.ds(0, grps - 1)], back_send.at[t])
        wait_for(out.at[:, t], back_recv.at[t])


def solution(mesh):
    doms, grps = mesh.shape["dom"], mesh.shape["grp"]

    def local(history, face_patch, refined, dest_slot, w_in, in_bias, w_out):
        per_dev, hist_len, block, cell_count = history.shape
        hid, ch = w_out.shape
        side = round(cell_count ** (1 / 3))
        plane = side * side
        width = 8 * side
        sizes = (doms, grps, side, hist_len, ch, hid)
        smem = pl.BlockSpec(memory_space=pltpu.SMEM)
        anywhere = pl.BlockSpec(memory_space=pl.ANY)
        vmem, dma = pltpu.VMEM, pltpu.SemaphoreType.DMA
        column = min(128, plane)
        return pl.pallas_call(
            functools.partial(surrogate, sizes),
            out_shape=jax.ShapeDtypeStruct((per_dev, 2, block, cell_count), BF16),
            in_specs=[smem, smem, smem, anywhere, anywhere, anywhere, pl.BlockSpec(memory_space=pltpu.VMEM)],
            out_specs=anywhere,
            scratch_shapes=[
                vmem((hist_len, per_dev, block, cell_count), BF16),
                vmem((hist_len, 2, block, cell_count), BF16),
                vmem((hist_len, 2, block, cell_count), BF16),
                vmem((hist_len, per_dev, block, cell_count), BF16),
                vmem((hist_len, per_dev, grps, block, plane), BF16),
                vmem((per_dev, grps, block, plane), BF16),
                vmem((per_dev, grps, block, plane), BF16),
                *[vmem((7, grps, block, plane), BF16) for _ in range(4)],
                *[vmem((3, ch, width), BF16) for _ in range(2)],
                vmem(w_in.shape, BF16),
                vmem(w_out.shape, BF16),
                vmem((hid, w_in.shape[0]), BF16),
                vmem((ch, hid), BF16),
                vmem((hid, column), F32),
                vmem((w_in.shape[0], per_dev * plane), BF16),
                vmem((hid, per_dev * plane), F32),
                vmem((plane, plane), BF16),
                vmem((2, plane, width), BF16),
                vmem((width, plane), BF16),
                dma((hist_len + 2,)),
                dma((hist_len, 2)),
                dma((hist_len, 2)),
                dma((hist_len,)),
                dma((hist_len,)),
                dma((2,)),
                dma((2,)),
                dma((2, 6)),
                dma((2, 6)),
            ],
            compiler_params=pltpu.CompilerParams(
                collective_id=0, has_side_effects=True, vmem_limit_bytes=60 * 2**20),
            name="surrogate",
        )(dest_slot, face_patch.T, refined, history, w_in, w_out, in_bias.reshape(1, hid))

    placed = (P("dom", None, "grp", None), P(), P(), P(), P(), P(), P())
    return jax.shard_map(
        local, mesh=mesh, in_specs=placed, out_specs=P("dom", None, "grp", None), check_vma=False
    )
```

```python
import functools

import jax
import jax.numpy as jnp
from jax import lax
from jax.experimental import pallas as pl
from jax.experimental.pallas import tpu as pltpu
from jax.sharding import PartitionSpec as P

MESH = pl.DeviceIdType.MESH
F32, BF16 = jnp.float32, jnp.bfloat16


def surrogate(sizes, dest, face, refined, hist, w_in, w_out, bias, out, own, stage, moved, mine, cells, last, stage_last,
              moved_last, state1, state2, xm1, xp1, xm2, xp2, edge1, edge2, w_raw, wo_raw, wt, wot, bcol, base1, base2,
              adj, pick, place, load_sem, mig_send, mig_recv, go_send, go_recv, back_send, back_recv, halo_send,
              halo_recv):
    doms, grps, side, hist_len, ch, hid = sizes
    plane = side * side
    block = ch // grps
    oldest = hist_len - 1
    d, g = lax.axis_index("dom"), lax.axis_index("grp")
    left, right = d - 1, d + 1
    has_left, has_right = d > 0, d < doms - 1
    up, down = lax.rem(g + 1, grps), lax.rem(g + grps - 1, grps)
    my_plane = down

    def wait_for(ref, sem):
        pltpu.make_async_copy(ref, ref, sem).wait()

    def remote(src, dst, send_sem, recv_sem, to):
        return pltpu.make_async_remote_copy(
            src_ref=src, dst_ref=dst, send_sem=send_sem, recv_sem=recv_sem, device_id=to, device_id_type=MESH)

    loads = [pltpu.make_async_copy(hist.at[:, k], own.at[k], load_sem.at[k]) for k in range(hist_len)]
    loads.append(pltpu.make_async_copy(w_in, w_raw, load_sem.at[hist_len]))
    loads.append(pltpu.make_async_copy(w_out, wo_raw, load_sem.at[hist_len + 1]))

    barrier = pltpu.get_barrier_semaphore()

    def greet(i, carry):
        pl.semaphore_signal(barrier, inc=1, device_id=(d, lax.rem(g + i, grps)), device_id_type=MESH)
        return carry

    lax.fori_loop(1, grps, greet, 0)
    for there, beside in ((has_left, left), (has_right, right)):
        @pl.when(there)
        def _(beside=beside):
            pl.semaphore_signal(barrier, inc=1, device_id=(beside, g), device_id_type=MESH)

            @pl.when(g < 2)
            def _():
                pl.semaphore_signal(barrier, inc=1, device_id=(beside, 1 - g), device_id_type=MESH)

    for load in loads:
        load.start()

    patches = 2 * doms
    cands = [lax.rem(2 * d + patches - 2 + i, patches) for i in range(6)]
    goals = [dest[c] for c in cands]
    go_left = jnp.where(goals[3] // 2 == d - 1, 1, 0)
    go_right = jnp.where(goals[3] // 2 == d + 1, 1, 0)
    origin, beside_slot, step_size = [], [], []
    for j in range(2):
        place_of = jnp.int32(0)
        owner = jnp.int32(0)
        for i in range(6):
            hit = goals[i] == 2 * d + j
            place_of = jnp.where(hit, i, place_of)
            owner = jnp.where(hit, cands[i], owner)
        origin.append(place_of)
        row = []
        for f in range(6):
            q = face[f, owner]
            pos = jnp.clip(dest[jnp.maximum(q, 0)] - 2 * (d - 1), 0, 5)
            row.append(jnp.where(q >= 0, pos, 6))
        beside_slot.append(row)
        step_size.append(1.0 - 0.5 * refined[owner].astype(F32))

    def placed(j, mine_of, from_left, from_right):
        at = origin[j]
        stays = jnp.where(at == 2, mine_of(0), mine_of(1))
        comes = jnp.where(at < 2, from_left, from_right)
        return jnp.where((at == 2) | (at == 3), stays, comes)

    for buf in (xm1, xp1, xm2, xp2):
        buf[6] = jnp.zeros(buf.shape[1:], BF16)
    for k in range(hist_len):
        loads[k].wait()
    beside_count = jnp.where(has_left, 1, 0) + jnp.where(has_right, 1, 0)
    pl.semaphore_wait(barrier, grps - 1 + beside_count * jnp.where(g < 2, 2, 1))

    def sent(src, dst, k):
        return [(has_right, remote(src.at[0], dst.at[0], mig_send.at[k, 0], mig_recv.at[k, 0], (right, g))),
                (has_left, remote(src.at[1], dst.at[1], mig_send.at[k, 1], mig_recv.at[k, 1], (left, g)))]

    def move(k):
        for to, which in enumerate((go_right, go_left)):
            stage[k, to] = jnp.where(which == 1, own[k, 1], own[k, 0])
        start_moves(stage.at[k], moved.at[k], k)

    def start_moves(src, dst, k):
        for there, copy in sent(src, dst, k):
            pl.when(there)(copy.start)

    def arrived(src, dst, k):
        (_, from_left), (_, from_right) = sent(src, dst, k)
        pl.when(has_left)(from_left.wait_recv)
        pl.when(has_right)(from_right.wait_recv)

    def lanes_of(device):
        return pl.ds(pl.multiple_of(lax.rem(device + grps - 1, grps) * plane, plane), plane)

    def far_first(i):
        half = lax.div(i, 2)
        return lax.rem(g + grps // 2 + jnp.where(lax.rem(i, 2) == 0, half, -half), grps)

    def spread_planes(src, dst, k):
        def send(i, carry):
            peer = far_first(i)
            remote(src.at[:, :, lanes_of(peer)], dst.at[:, g], go_send.at[k], go_recv.at[k], (d, peer)).start()
            return carry

        lax.fori_loop(1, grps, send, 0)
        pltpu.make_async_copy(src.at[:, :, lanes_of(g)], dst.at[:, g], go_recv.at[k]).start()

    def settle(k):
        arrived(stage.at[k], moved.at[k], k)
        for j in range(2):
            mine[k, j] = placed(j, lambda i: own[k, i], moved[k, 0], moved[k, 1])
        spread_planes(mine.at[k], cells.at[k], k)

    def wide(ref_value):
        return ref_value.astype(F32).reshape(ch, plane)

    move(0)
    spread_planes(own.at[oldest], last, oldest)
    for k in range(1, oldest):
        move(k)
    for k in range(oldest):
        settle(k)

    r = lax.broadcasted_iota(jnp.int32, (plane, plane), 0)
    c = lax.broadcasted_iota(jnp.int32, (plane, plane), 1)
    ry, rz, cy, cz = r // side, r % side, c // side, c % side
    beside_cell = ((ry == cy) & (jnp.abs(rz - cz) == 1)) | ((rz == cz) & (jnp.abs(ry - cy) == 1))
    adj[...] = jnp.where(r == c, -6.0, jnp.where(beside_cell, 1.0, 0.0)).astype(BF16)
    width = 8 * side

    def layer_cell(layer, k):
        along_y = jnp.where(layer == 0, k, plane - side + k)
        along_z = jnp.where(layer == 2, k * side, k * side + side - 1)
        return jnp.where(layer < 2, along_y, along_z)

    r = lax.broadcasted_iota(jnp.int32, (plane, width), 0)
    c = lax.broadcasted_iota(jnp.int32, (plane, width), 1)
    for j in range(2):
        hit = (r == layer_cell((c // side) % 4, c % side)) & (c // (4 * side) == j)
        pick[j] = jnp.where(hit, 1.0, 0.0).astype(BF16)
    r = lax.broadcasted_iota(jnp.int32, (width, plane), 0)
    c = lax.broadcasted_iota(jnp.int32, (width, plane), 1)
    layer = (r // side) % 4
    opposite = jnp.where(layer % 2 == 0, layer + 1, layer - 1)
    place[...] = jnp.where(c == layer_cell(opposite, r % side), 1.0, 0.0).astype(BF16)
    bcol[...] = jnp.broadcast_to(bias[...], (bcol.shape[1], hid)).T
    loads[hist_len].wait()
    loads[hist_len + 1].wait()
    for k in range(hist_len + 1):
        wt[:, k * ch:(k + 1) * ch] = w_raw[k * ch:(k + 1) * ch, :].astype(F32).T.astype(BF16)
    wot[...] = wo_raw[...].astype(F32).T.astype(BF16)

    wait_for(last, go_recv.at[oldest])
    for to, which in enumerate((go_right, go_left)):
        stage_last[to] = jnp.where(which == 1, last[1], last[0])
    start_moves(stage_last, moved_last, oldest)

    lane = lax.broadcasted_iota(jnp.int32, (ch, width), 1)
    lane_layer, lane_patch = (lane // side) % 4, lane // (4 * side)

    def halo_copies(t, state, xm, xp, j):
        sem = lambda i: (halo_send.at[t, 5 * j + i], halo_recv.at[t, 5 * j + i])
        return (remote(state.at[j], xm.at[2 + j], *sem(0), (d, up)),
                remote(state.at[j], xp.at[2 + j], *sem(1), (d, down)))

    def rim_copies(t, state, buf, j):
        sem = lambda i: (halo_send.at[t, 5 * j + i], halo_recv.at[t, 5 * j + i])
        return ((has_right, remote(state.at[j], buf.at[j], *sem(2), (right, 1 - g))),
                (has_left, remote(state.at[j], buf.at[4 + j], *sem(3), (left, 1 - g))))

    def edge_copies(t, edge):
        return ((has_right, remote(edge.at[1], edge.at[0], halo_send.at[t, 4], halo_recv.at[t, 4], (right, g))),
                (has_left, remote(edge.at[1], edge.at[2], halo_send.at[t, 9], halo_recv.at[t, 9], (left, g))))

    def start_halo(t, state, xm, xp, j):
        for at, buf in ((0, xm), (1, xp)):
            for there, copy in rim_copies(t, state, buf, j):
                pl.when((g == at) & there)(copy.start)
        for copy in halo_copies(t, state, xm, xp, j):
            copy.start()

    def start_edges(t, state, edge):
        edges = sum(jnp.dot(wide(state[j]).astype(BF16), pick[j], preferred_element_type=F32) for j in range(2))
        edge[1] = edges.astype(BF16)
        for there, copy in edge_copies(t, edge):
            pl.when(there)(copy.start)

    def finish_halo(t, state, xm, xp, edge):
        for j in range(2):
            for copy in halo_copies(t, state, xm, xp, j):
                copy.wait()
            for at, out_buf, in_buf in ((0, xm, xp), (1, xp, xm)):
                (_, to_right), (_, to_left) = rim_copies(t, state, out_buf, j)
                (_, from_left), (_, from_right) = rim_copies(t, state, in_buf, j)
                for there, copy in ((has_right, to_right), (has_left, to_left)):
                    pl.when((g == at) & there)(copy.wait_send)
                for there, copy in ((has_left, from_left), (has_right, from_right)):
                    pl.when((g == at) & there)(copy.wait_recv)
        (_, right_edge), (_, left_edge) = edge_copies(t, edge)
        pl.when(has_right)(right_edge.wait_send)
        pl.when(has_left)(left_edge.wait_send)
        pl.when(has_left)(right_edge.wait_recv)
        pl.when(has_right)(left_edge.wait_recv)

    def laplace(state, xm, xp, edge, j):
        near = jnp.dot(wide(state[j]).astype(BF16), adj[...], preferred_element_type=F32)
        slots = beside_slot[j]
        wanted = jnp.where(lane_layer == 0, slots[3], jnp.where(lane_layer == 1, slots[2], jnp.where(
            lane_layer == 2, slots[5], slots[4])))
        faces = jnp.zeros((ch, width), F32)
        for i in range(3):
            faces = jnp.where(wanted == 2 * i + lane_patch, edge[i].astype(F32), faces)
        near = near + jnp.dot(faces.astype(BF16), place[...], preferred_element_type=F32)
        before = xm[jnp.where(my_plane == 0, slots[0], 2 + j)]
        after = xp[jnp.where(my_plane == grps - 1, slots[1], 2 + j)]
        return (near + wide(before) + wide(after)).astype(BF16)

    def times(k, rows):
        return jnp.dot(wt[:, k * ch:(k + 1) * ch], rows, preferred_element_type=F32)

    cols = [slice(j * plane, (j + 1) * plane) for j in range(2)]

    def next_state(pre, start, j):
        hidden = (pre / (1.0 + jnp.exp(-pre))).astype(BF16)
        update = jnp.dot(wot[...], hidden, preferred_element_type=F32).astype(BF16)
        fresh = start + step_size[j] * update.astype(F32)
        return fresh.reshape(grps, block, plane).astype(BF16)

    def send_back(t, state):
        def send(i, carry):
            peer = far_first(i)
            remote(state.at[:, peer], out.at[:, t, :, lanes_of(g)], back_send.at[t], back_recv.at[t],
                   (d, peer)).start()
            return carry

        lax.fori_loop(1, grps, send, 0)
        pltpu.make_async_copy(state.at[:, g], out.at[:, t, :, lanes_of(g)], back_recv.at[t]).start()

    newest = cells.at[0]
    wait_for(newest, go_recv.at[0])
    for j in range(2):
        start_halo(0, newest, xm1, xp1, j)
    start_edges(0, newest, edge1)
    wide_bias = jnp.concatenate([bcol[...]] * (plane // bcol.shape[1]), 1)
    for j in range(2):
        rows = wide(newest[j]).astype(BF16)
        base1[:, cols[j]] = wide_bias + times(0, rows)
        base2[:, cols[j]] = wide_bias + times(1, rows)
    arrived(stage_last, moved_last, oldest)
    for j in range(2):
        rows = placed(j, lambda i: last[i].astype(F32), moved_last[0].astype(F32), moved_last[1].astype(F32))
        base1[:, cols[j]] += times(oldest, rows.reshape(ch, plane).astype(BF16))
    finish_halo(0, newest, xm1, xp1, edge1)
    for j in range(2):
        base1[:, cols[j]] += times(hist_len, laplace(newest, xm1, xp1, edge1, j))
    for k in range(1, oldest - 1):
        wait_for(cells.at[k], go_recv.at[k])
        for j in range(2):
            rows = wide(cells[k, j]).astype(BF16)
            base1[:, cols[j]] += times(k, rows)
            base2[:, cols[j]] += times(k + 1, rows)
    wait_for(cells.at[oldest - 1], go_recv.at[oldest - 1])
    for j in range(2):
        pre = base1[:, cols[j]] + times(oldest - 1, wide(cells[oldest - 1, j]).astype(BF16))
        state1[j] = next_state(pre, wide(newest[j]), j)
        start_halo(1, state1, xm2, xp2, j)
    start_edges(1, state1, edge2)
    send_back(0, state1)
    for j in range(2):
        more = times(oldest, wide(cells[oldest - 1, j]).astype(BF16)) + times(0, wide(state1[j]).astype(BF16))
        base2[:, cols[j]] += more
    finish_halo(1, state1, xm2, xp2, edge2)
    for j in range(2):
        pre = base2[:, cols[j]] + times(hist_len, laplace(state1, xm2, xp2, edge2, j))
        state2[j] = next_state(pre, wide(state1[j]), j)
    send_back(1, state2)

    for k in range(hist_len):
        src, dst = (stage_last, moved_last) if k == oldest else (stage.at[k], moved.at[k])
        for there, copy in sent(src, dst, k):
            pl.when(there)(copy.wait_send)
        wait_for(last.at[:, pl.ds(0, grps - 1)], go_send.at[k])
    for t in range(2):
        wait_for(state1.at[:, pl.ds(0, grps - 1)], back_send.at[t])
        wait_for(out.at[:, t], back_recv.at[t])


def solution(mesh):
    doms, grps = mesh.shape["dom"], mesh.shape["grp"]

    def local(history, face_patch, refined, dest_slot, w_in, in_bias, w_out):
        per_dev, hist_len, block, cell_count = history.shape
        hid, ch = w_out.shape
        side = round(cell_count ** (1 / 3))
        plane = side * side
        width = 8 * side
        sizes = (doms, grps, side, hist_len, ch, hid)
        smem = pl.BlockSpec(memory_space=pltpu.SMEM)
        anywhere = pl.BlockSpec(memory_space=pl.ANY)
        vmem, dma = pltpu.VMEM, pltpu.SemaphoreType.DMA
        column = min(128, plane)
        states = pl.pallas_call(
            functools.partial(surrogate, sizes),
            out_shape=pltpu.VMEM((per_dev, 2, block, cell_count), BF16),
            in_specs=[smem, smem, smem, anywhere, anywhere, anywhere, pl.BlockSpec(memory_space=pltpu.VMEM)],
            out_specs=pl.BlockSpec(memory_space=pltpu.VMEM),
            scratch_shapes=[
                vmem((hist_len, per_dev, block, cell_count), BF16),
                *[vmem((hist_len - 1, 2, block, cell_count), BF16) for _ in range(3)],
                vmem((hist_len - 1, per_dev, grps, block, plane), BF16),
                *[vmem((2, grps, block, plane), BF16) for _ in range(3)],
                vmem((per_dev, grps, block, plane), BF16),
                vmem((per_dev, grps, block, plane), BF16),
                *[vmem((7, grps, block, plane), BF16) for _ in range(4)],
                *[vmem((3, ch, width), BF16) for _ in range(2)],
                vmem(w_in.shape, BF16),
                vmem(w_out.shape, BF16),
                vmem((hid, w_in.shape[0]), BF16),
                vmem((ch, hid), BF16),
                vmem((hid, column), F32),
                *[vmem((hid, per_dev * plane), F32) for _ in range(2)],
                vmem((plane, plane), BF16),
                vmem((2, plane, width), BF16),
                vmem((width, plane), BF16),
                dma((hist_len + 2,)),
                dma((hist_len, 2)),
                dma((hist_len, 2)),
                dma((hist_len,)),
                dma((hist_len,)),
                dma((2,)),
                dma((2,)),
                dma((2, 10)),
                dma((2, 10)),
            ],
            compiler_params=pltpu.CompilerParams(
                collective_id=0, has_side_effects=True, vmem_limit_bytes=60 * 2**20),
            name="surrogate",
        )(dest_slot, face_patch.T, refined, history, w_in, w_out, in_bias.reshape(1, hid))
        return states

    placed = (P("dom", None, "grp", None), P(), P(), P(), P(), P(), P())
    return jax.shard_map(
        local, mesh=mesh, in_specs=placed, out_specs=P("dom", None, "grp", None), check_vma=False
    )
```

```python
import functools

import jax
import jax.numpy as jnp
from jax import lax
from jax.experimental import pallas as pl
from jax.experimental.pallas import tpu as pltpu
from jax.sharding import PartitionSpec as P

MESH = pl.DeviceIdType.MESH
F32, BF16 = jnp.float32, jnp.bfloat16


def surrogate(sizes, dest_in, face_in, refined_in, hist, w_in, w_out, bias_in, out, dest, face, refined, bias, own, stage, moved, mine, cells, last, stage_last,
              moved_last, state1, state2, xm1, xp1, xm2, xp2, edge1, edge2, w_raw, wo_raw, wt, wot, bcol, base1, base2,
              adj, pick, place, load_sem, mig_send, mig_recv, go_send, go_recv, back_send, back_recv, halo_send,
              halo_recv):
    doms, grps, side, hist_len, ch, hid = sizes
    plane = side * side
    block = ch // grps
    late = hist_len - 2
    d, g = lax.axis_index("dom"), lax.axis_index("grp")
    left, right = d - 1, d + 1
    has_left, has_right = d > 0, d < doms - 1
    up, down = lax.rem(g + 1, grps), lax.rem(g + grps - 1, grps)
    my_plane = down

    def wait_for(ref, sem):
        pltpu.make_async_copy(ref, ref, sem).wait()

    def remote(src, dst, send_sem, recv_sem, to):
        return pltpu.make_async_remote_copy(
            src_ref=src, dst_ref=dst, send_sem=send_sem, recv_sem=recv_sem, device_id=to, device_id_type=MESH)

    loads = [pltpu.make_async_copy(hist.at[:, k], own.at[k], load_sem.at[k]) for k in range(hist_len)]
    loads.append(pltpu.make_async_copy(w_in, w_raw, load_sem.at[hist_len]))
    loads.append(pltpu.make_async_copy(w_out, wo_raw, load_sem.at[hist_len + 1]))
    small = ((dest_in, dest), (face_in, face), (refined_in, refined), (bias_in, bias))
    tables = [pltpu.make_async_copy(src, dst, load_sem.at[hist_len + 2 + i]) for i, (src, dst) in enumerate(small)]

    def far_first(i):
        half = lax.div(i, 2)
        return lax.rem(g + grps // 2 + jnp.where(lax.rem(i, 2) == 0, half, -half), grps)

    barrier = pltpu.get_barrier_semaphore()

    def greet(i, carry):
        pl.semaphore_signal(barrier, inc=1, device_id=(d, far_first(i)), device_id_type=MESH)
        return carry

    lax.fori_loop(1, grps, greet, 0)
    for there, beside in ((has_left, left), (has_right, right)):
        @pl.when(there)
        def _(beside=beside):
            pl.semaphore_signal(barrier, inc=1, device_id=(beside, g), device_id_type=MESH)

            @pl.when(g < 2)
            def _():
                pl.semaphore_signal(barrier, inc=1, device_id=(beside, 1 - g), device_id_type=MESH)

    for load in tables + loads:
        load.start()
    for table in tables:
        table.wait()

    patches = 2 * doms
    cands = [lax.rem(2 * d + patches - 2 + i, patches) for i in range(6)]
    goals = [dest[c] for c in cands]
    go_left = jnp.where(goals[3] // 2 == d - 1, 1, 0)
    go_right = jnp.where(goals[3] // 2 == d + 1, 1, 0)
    origin, beside_slot, step_size = [], [], []
    for j in range(2):
        place_of = jnp.int32(0)
        owner = jnp.int32(0)
        for i in range(6):
            hit = goals[i] == 2 * d + j
            place_of = jnp.where(hit, i, place_of)
            owner = jnp.where(hit, cands[i], owner)
        origin.append(place_of)
        row = []
        for f in range(6):
            q = face[f, owner]
            pos = jnp.clip(dest[jnp.maximum(q, 0)] - 2 * (d - 1), 0, 5)
            row.append(jnp.where(q >= 0, pos, 6))
        beside_slot.append(row)
        step_size.append(1.0 - 0.5 * refined[owner].astype(F32))

    def placed(j, mine_of, from_left, from_right):
        at = origin[j]
        stays = jnp.where(at == 2, mine_of(0), mine_of(1))
        comes = jnp.where(at < 2, from_left, from_right)
        return jnp.where((at == 2) | (at == 3), stays, comes)

    for buf in (xm1, xp1, xm2, xp2):
        buf[6] = jnp.zeros(buf.shape[1:], BF16)
    for k in range(hist_len):
        loads[k].wait()
    beside_count = jnp.where(has_left, 1, 0) + jnp.where(has_right, 1, 0)
    pl.semaphore_wait(barrier, grps - 1 + beside_count * jnp.where(g < 2, 2, 1))

    def sent(src, dst, k):
        return [(has_right, remote(src.at[0], dst.at[0], mig_send.at[k, 0], mig_recv.at[k, 0], (right, g))),
                (has_left, remote(src.at[1], dst.at[1], mig_send.at[k, 1], mig_recv.at[k, 1], (left, g)))]

    def move(k):
        for to, which in enumerate((go_right, go_left)):
            stage[k, to] = jnp.where(which == 1, own[k, 1], own[k, 0])
        start_moves(stage.at[k], moved.at[k], k)

    def start_moves(src, dst, k):
        for there, copy in sent(src, dst, k):
            pl.when(there)(copy.start)

    def arrived(src, dst, k):
        (_, from_left), (_, from_right) = sent(src, dst, k)
        pl.when(has_left)(from_left.wait_recv)
        pl.when(has_right)(from_right.wait_recv)

    def lanes_of(device):
        return pl.ds(pl.multiple_of(lax.rem(device + grps - 1, grps) * plane, plane), plane)

    def spread_planes(src, dst, k):
        def send(i, carry):
            peer = far_first(i)
            remote(src.at[:, :, lanes_of(peer)], dst.at[:, g], go_send.at[k], go_recv.at[k], (d, peer)).start()
            return carry

        lax.fori_loop(1, grps, send, 0)
        pltpu.make_async_copy(src.at[:, :, lanes_of(g)], dst.at[:, g], go_recv.at[k]).start()

    def settle(k):
        arrived(stage.at[k], moved.at[k], k)
        for j in range(2):
            mine[k, j] = placed(j, lambda i: own[k, i], moved[k, 0], moved[k, 1])
        spread_planes(mine.at[k], cells.at[k], k)

    def wide(ref_value):
        return ref_value.astype(F32).reshape(ch, plane)

    move(0)
    spread_planes(own.at[hist_len - 1], last.at[1], hist_len - 1)
    for k in range(1, late):
        move(k)
    spread_planes(own.at[late], last.at[0], late)
    for k in range(late):
        settle(k)

    r = lax.broadcasted_iota(jnp.int32, (plane, plane), 0)
    c = lax.broadcasted_iota(jnp.int32, (plane, plane), 1)
    ry, rz, cy, cz = r // side, r % side, c // side, c % side
    beside_cell = ((ry == cy) & (jnp.abs(rz - cz) == 1)) | ((rz == cz) & (jnp.abs(ry - cy) == 1))
    adj[...] = jnp.where(r == c, -6.0, jnp.where(beside_cell, 1.0, 0.0)).astype(BF16)
    width = 8 * side

    def layer_cell(layer, k):
        along_y = jnp.where(layer == 0, k, plane - side + k)
        along_z = jnp.where(layer == 2, k * side, k * side + side - 1)
        return jnp.where(layer < 2, along_y, along_z)

    r = lax.broadcasted_iota(jnp.int32, (plane, width), 0)
    c = lax.broadcasted_iota(jnp.int32, (plane, width), 1)
    for j in range(2):
        hit = (r == layer_cell((c // side) % 4, c % side)) & (c // (4 * side) == j)
        pick[j] = jnp.where(hit, 1.0, 0.0).astype(BF16)
    r = lax.broadcasted_iota(jnp.int32, (width, plane), 0)
    c = lax.broadcasted_iota(jnp.int32, (width, plane), 1)
    layer = (r // side) % 4
    opposite = jnp.where(layer % 2 == 0, layer + 1, layer - 1)
    place[...] = jnp.where(c == layer_cell(opposite, r % side), 1.0, 0.0).astype(BF16)
    bcol[...] = jnp.broadcast_to(bias[...], (bcol.shape[1], hid)).T
    for k in (hist_len - 1, late):
        r = k - late
        wait_for(last.at[r], go_recv.at[k])
        for to, which in enumerate((go_right, go_left)):
            stage_last[r, to] = jnp.where(which == 1, last[r, 1], last[r, 0])
        start_moves(stage_last.at[r], moved_last.at[r], k)
    loads[hist_len].wait()
    loads[hist_len + 1].wait()
    for k in range(hist_len + 1):
        wt[:, k * ch:(k + 1) * ch] = w_raw[k * ch:(k + 1) * ch, :].astype(F32).T.astype(BF16)
    wot[...] = wo_raw[...].astype(F32).T.astype(BF16)

    lane = lax.broadcasted_iota(jnp.int32, (ch, width), 1)
    lane_layer, lane_patch = (lane // side) % 4, lane // (4 * side)

    def halo_copies(t, state, xm, xp, j):
        sem = lambda i: (halo_send.at[t, 5 * j + i], halo_recv.at[t, 5 * j + i])
        return (remote(state.at[j], xm.at[2 + j], *sem(0), (d, up)),
                remote(state.at[j], xp.at[2 + j], *sem(1), (d, down)))

    def rim_copies(t, state, buf, j):
        sem = lambda i: (halo_send.at[t, 5 * j + i], halo_recv.at[t, 5 * j + i])
        return ((has_right, remote(state.at[j], buf.at[j], *sem(2), (right, 1 - g))),
                (has_left, remote(state.at[j], buf.at[4 + j], *sem(3), (left, 1 - g))))

    def edge_copies(t, edge):
        return ((has_right, remote(edge.at[1], edge.at[0], halo_send.at[t, 4], halo_recv.at[t, 4], (right, g))),
                (has_left, remote(edge.at[1], edge.at[2], halo_send.at[t, 9], halo_recv.at[t, 9], (left, g))))

    def start_halo(t, state, xm, xp, j):
        for at, buf in ((0, xm), (1, xp)):
            for there, copy in rim_copies(t, state, buf, j):
                pl.when((g == at) & there)(copy.start)
        for copy in halo_copies(t, state, xm, xp, j):
            copy.start()

    def start_edges(t, state, edge):
        edges = sum(jnp.dot(wide(state[j]).astype(BF16), pick[j], preferred_element_type=F32) for j in range(2))
        edge[1] = edges.astype(BF16)
        for there, copy in edge_copies(t, edge):
            pl.when(there)(copy.start)

    def finish_halo(t, state, xm, xp, edge):
        for j in range(2):
            for copy in halo_copies(t, state, xm, xp, j):
                copy.wait()
            for at, out_buf, in_buf in ((0, xm, xp), (1, xp, xm)):
                (_, to_right), (_, to_left) = rim_copies(t, state, out_buf, j)
                (_, from_left), (_, from_right) = rim_copies(t, state, in_buf, j)
                for there, copy in ((has_right, to_right), (has_left, to_left)):
                    pl.when((g == at) & there)(copy.wait_send)
                for there, copy in ((has_left, from_left), (has_right, from_right)):
                    pl.when((g == at) & there)(copy.wait_recv)
        (_, right_edge), (_, left_edge) = edge_copies(t, edge)
        pl.when(has_right)(right_edge.wait_send)
        pl.when(has_left)(left_edge.wait_send)
        pl.when(has_left)(right_edge.wait_recv)
        pl.when(has_right)(left_edge.wait_recv)

    def laplace(state, xm, xp, edge, j):
        near = jnp.dot(wide(state[j]).astype(BF16), adj[...], preferred_element_type=F32)
        slots = beside_slot[j]
        wanted = jnp.where(lane_layer == 0, slots[3], jnp.where(lane_layer == 1, slots[2], jnp.where(
            lane_layer == 2, slots[5], slots[4])))
        faces = jnp.zeros((ch, width), F32)
        for i in range(3):
            faces = jnp.where(wanted == 2 * i + lane_patch, edge[i].astype(F32), faces)
        near = near + jnp.dot(faces.astype(BF16), place[...], preferred_element_type=F32)
        before = xm[jnp.where(my_plane == 0, slots[0], 2 + j)]
        after = xp[jnp.where(my_plane == grps - 1, slots[1], 2 + j)]
        return (near + wide(before) + wide(after)).astype(BF16)

    def times(k, rows):
        return jnp.dot(wt[:, k * ch:(k + 1) * ch], rows, preferred_element_type=F32)

    cols = [slice(j * plane, (j + 1) * plane) for j in range(2)]

    def next_state(pre, start, j):
        hidden = (pre / (1.0 + jnp.exp(-pre))).astype(BF16)
        update = jnp.dot(wot[...], hidden, preferred_element_type=F32).astype(BF16)
        fresh = start + step_size[j] * update.astype(F32)
        return fresh.reshape(grps, block, plane).astype(BF16)

    def send_back(t, state):
        def send(i, carry):
            peer = far_first(i)
            remote(state.at[:, peer], out.at[:, t, :, lanes_of(g)], back_send.at[t], back_recv.at[t],
                   (d, peer)).start()
            return carry

        lax.fori_loop(1, grps, send, 0)
        pltpu.make_async_copy(state.at[:, g], out.at[:, t, :, lanes_of(g)], back_recv.at[t]).start()

    newest = cells.at[0]
    wait_for(newest, go_recv.at[0])
    for j in range(2):
        start_halo(0, newest, xm1, xp1, j)
    start_edges(0, newest, edge1)
    wide_bias = jnp.concatenate([bcol[...]] * (plane // bcol.shape[1]), 1)
    for j in range(2):
        rows = wide(newest[j]).astype(BF16)
        base1[:, cols[j]] = wide_bias + times(0, rows)
        base2[:, cols[j]] = wide_bias + times(1, rows)
    for k in (hist_len - 1, late):
        r = k - late
        arrived(stage_last.at[r], moved_last.at[r], k)
        for j in range(2):
            rows = placed(j, lambda i: last[r, i].astype(F32), moved_last[r, 0].astype(F32), moved_last[r, 1].astype(F32))
            rows = rows.reshape(ch, plane).astype(BF16)
            base1[:, cols[j]] += times(k, rows)
            if k + 1 < hist_len:
                base2[:, cols[j]] += times(k + 1, rows)
    finish_halo(0, newest, xm1, xp1, edge1)
    for j in range(2):
        base1[:, cols[j]] += times(hist_len, laplace(newest, xm1, xp1, edge1, j))
    for k in range(1, late):
        wait_for(cells.at[k], go_recv.at[k])
    for j in range(2):
        pre = base1[:, cols[j]]
        for k in range(1, late):
            pre = pre + times(k, wide(cells[k, j]).astype(BF16))
        state1[j] = next_state(pre, wide(newest[j]), j)
        start_halo(1, state1, xm2, xp2, j)
    start_edges(1, state1, edge2)
    send_back(0, state1)
    for j in range(2):
        more = times(0, wide(state1[j]).astype(BF16))
        for k in range(1, late):
            more = more + times(k + 1, wide(cells[k, j]).astype(BF16))
        base2[:, cols[j]] += more
    finish_halo(1, state1, xm2, xp2, edge2)
    for j in range(2):
        pre = base2[:, cols[j]] + times(hist_len, laplace(state1, xm2, xp2, edge2, j))
        state2[j] = next_state(pre, wide(state1[j]), j)
    send_back(1, state2)

    for k in range(hist_len):
        src, dst = (stage.at[k], moved.at[k]) if k < late else (stage_last.at[k - late], moved_last.at[k - late])
        for there, copy in sent(src, dst, k):
            pl.when(there)(copy.wait_send)
        wait_for(last.at[0, :, pl.ds(0, grps - 1)], go_send.at[k])
    for t in range(2):
        wait_for(state1.at[:, pl.ds(0, grps - 1)], back_send.at[t])
        wait_for(out.at[:, t], back_recv.at[t])


def solution(mesh):
    doms, grps = mesh.shape["dom"], mesh.shape["grp"]

    def local(history, face_patch, refined, dest_slot, w_in, in_bias, w_out):
        per_dev, hist_len, block, cell_count = history.shape
        hid, ch = w_out.shape
        side = round(cell_count ** (1 / 3))
        plane = side * side
        width = 8 * side
        sizes = (doms, grps, side, hist_len, ch, hid)
        anywhere = pl.BlockSpec(memory_space=pl.ANY)
        vmem, dma = pltpu.VMEM, pltpu.SemaphoreType.DMA
        column = min(128, plane)
        states = pl.pallas_call(
            functools.partial(surrogate, sizes),
            out_shape=pltpu.VMEM((per_dev, 2, block, cell_count), BF16),
            in_specs=[anywhere] * 7,
            out_specs=pl.BlockSpec(memory_space=pltpu.VMEM),
            scratch_shapes=[
                pltpu.SMEM(dest_slot.shape, jnp.int32),
                pltpu.SMEM(face_patch.shape[::-1], jnp.int32),
                pltpu.SMEM(refined.shape, jnp.int32),
                vmem((1, hid), F32),
                vmem((hist_len, per_dev, block, cell_count), BF16),
                *[vmem((hist_len - 2, 2, block, cell_count), BF16) for _ in range(3)],
                vmem((hist_len - 2, per_dev, grps, block, plane), BF16),
                *[vmem((2, 2, grps, block, plane), BF16) for _ in range(3)],
                vmem((per_dev, grps, block, plane), BF16),
                vmem((per_dev, grps, block, plane), BF16),
                *[vmem((7, grps, block, plane), BF16) for _ in range(4)],
                *[vmem((3, ch, width), BF16) for _ in range(2)],
                vmem(w_in.shape, BF16),
                vmem(w_out.shape, BF16),
                vmem((hid, w_in.shape[0]), BF16),
                vmem((ch, hid), BF16),
                vmem((hid, column), F32),
                *[vmem((hid, per_dev * plane), F32) for _ in range(2)],
                vmem((plane, plane), BF16),
                vmem((2, plane, width), BF16),
                vmem((width, plane), BF16),
                dma((hist_len + 6,)),
                dma((hist_len, 2)),
                dma((hist_len, 2)),
                dma((hist_len,)),
                dma((hist_len,)),
                dma((2,)),
                dma((2,)),
                dma((2, 10)),
                dma((2, 10)),
            ],
            compiler_params=pltpu.CompilerParams(
                collective_id=0, has_side_effects=True, vmem_limit_bytes=60 * 2**20),
            name="surrogate",
        )(dest_slot, face_patch.T, refined, history, w_in, w_out, in_bias.reshape(1, hid))
        return states

    placed = (P("dom", None, "grp", None), P(), P(), P(), P(), P(), P())
    return jax.shard_map(
        local, mesh=mesh, in_specs=placed, out_specs=P("dom", None, "grp", None), check_vma=False
    )
```

```python
import functools

import jax
import jax.numpy as jnp
from jax import lax
from jax.experimental import pallas as pl
from jax.experimental.pallas import tpu as pltpu
from jax.sharding import PartitionSpec as P

MESH = pl.DeviceIdType.MESH
F32, BF16 = jnp.float32, jnp.bfloat16


def surrogate(sizes, dest_in, face_in, refined_in, hist, w_in, w_out, bias_in, out, dest, face, refined, bias, own, stage, moved, mine, cells, last, stage_last,
              moved_last, state1, state2, xm1, xp1, xm2, xp2, edge1, edge2, w_raw, wo_raw, wt, wot, bcol, base1, base2,
              adj, pick, place, load_sem, mig_send, mig_recv, go_send, go_recv, back_send, back_recv, halo_send,
              halo_recv):
    doms, grps, side, hist_len, ch, hid = sizes
    plane = side * side
    block = ch // grps
    late = hist_len - 2
    d, g = lax.axis_index("dom"), lax.axis_index("grp")
    left, right = d - 1, d + 1
    has_left, has_right = d > 0, d < doms - 1
    up, down = lax.rem(g + 1, grps), lax.rem(g + grps - 1, grps)
    my_plane = down

    def wait_for(ref, sem):
        pltpu.make_async_copy(ref, ref, sem).wait()

    def remote(src, dst, send_sem, recv_sem, to):
        return pltpu.make_async_remote_copy(
            src_ref=src, dst_ref=dst, send_sem=send_sem, recv_sem=recv_sem, device_id=to, device_id_type=MESH)

    loads = [pltpu.make_async_copy(hist.at[:, k], own.at[k], load_sem.at[k]) for k in range(hist_len)]
    loads.append(pltpu.make_async_copy(w_in, w_raw, load_sem.at[hist_len]))
    loads.append(pltpu.make_async_copy(w_out, wo_raw, load_sem.at[hist_len + 1]))
    small = ((dest_in, dest), (face_in, face), (refined_in, refined), (bias_in, bias))
    tables = [pltpu.make_async_copy(src, dst, load_sem.at[hist_len + 2 + i]) for i, (src, dst) in enumerate(small)]

    def far_first(i):
        half = lax.div(i, 2)
        return lax.rem(g + grps // 2 + jnp.where(lax.rem(i, 2) == 0, half, -half), grps)

    first = [loads[0]] + loads[late:hist_len]
    for load in first:
        load.start()

    barrier = pltpu.get_barrier_semaphore()

    def greet(i, carry):
        pl.semaphore_signal(barrier, inc=1, device_id=(d, far_first(i)), device_id_type=MESH)
        return carry

    lax.fori_loop(1, grps, greet, 0)
    for there, beside in ((has_left, left), (has_right, right)):
        @pl.when(there)
        def _(beside=beside):
            pl.semaphore_signal(barrier, inc=1, device_id=(beside, g), device_id_type=MESH)

            @pl.when(g < 2)
            def _():
                pl.semaphore_signal(barrier, inc=1, device_id=(beside, 1 - g), device_id_type=MESH)

    for load in tables + loads[1:late] + loads[hist_len:]:
        load.start()
    for table in tables:
        table.wait()

    patches = 2 * doms
    cands = [lax.rem(2 * d + patches - 2 + i, patches) for i in range(6)]
    goals = [dest[c] for c in cands]
    go_left = jnp.where(goals[3] // 2 == d - 1, 1, 0)
    go_right = jnp.where(goals[3] // 2 == d + 1, 1, 0)
    origin, beside_slot, step_size = [], [], []
    for j in range(2):
        place_of = jnp.int32(0)
        owner = jnp.int32(0)
        for i in range(6):
            hit = goals[i] == 2 * d + j
            place_of = jnp.where(hit, i, place_of)
            owner = jnp.where(hit, cands[i], owner)
        origin.append(place_of)
        row = []
        for f in range(6):
            q = face[f, owner]
            pos = jnp.clip(dest[jnp.maximum(q, 0)] - 2 * (d - 1), 0, 5)
            row.append(jnp.where(q >= 0, pos, 6))
        beside_slot.append(row)
        step_size.append(1.0 - 0.5 * refined[owner].astype(F32))

    def placed(j, mine_of, from_left, from_right):
        at = origin[j]
        stays = jnp.where(at == 2, mine_of(0), mine_of(1))
        comes = jnp.where(at < 2, from_left, from_right)
        return jnp.where((at == 2) | (at == 3), stays, comes)

    for buf in (xm1, xp1, xm2, xp2):
        buf[6] = jnp.zeros(buf.shape[1:], BF16)
    for load in first:
        load.wait()
    beside_count = jnp.where(has_left, 1, 0) + jnp.where(has_right, 1, 0)
    pl.semaphore_wait(barrier, grps - 1 + beside_count * jnp.where(g < 2, 2, 1))

    def sent(src, dst, k):
        return [(has_right, remote(src.at[0], dst.at[0], mig_send.at[k, 0], mig_recv.at[k, 0], (right, g))),
                (has_left, remote(src.at[1], dst.at[1], mig_send.at[k, 1], mig_recv.at[k, 1], (left, g)))]

    def move(k):
        for to, which in enumerate((go_right, go_left)):
            stage[k, to] = jnp.where(which == 1, own[k, 1], own[k, 0])
        start_moves(stage.at[k], moved.at[k], k)

    def start_moves(src, dst, k):
        for there, copy in sent(src, dst, k):
            pl.when(there)(copy.start)

    def arrived(src, dst, k):
        (_, from_left), (_, from_right) = sent(src, dst, k)
        pl.when(has_left)(from_left.wait_recv)
        pl.when(has_right)(from_right.wait_recv)

    def lanes_of(device):
        return pl.ds(pl.multiple_of(lax.rem(device + grps - 1, grps) * plane, plane), plane)

    def spread_planes(src, dst, k):
        def send(i, carry):
            peer = far_first(i)
            remote(src.at[:, :, lanes_of(peer)], dst.at[:, g], go_send.at[k], go_recv.at[k], (d, peer)).start()
            return carry

        lax.fori_loop(1, grps, send, 0)
        pltpu.make_async_copy(src.at[:, :, lanes_of(g)], dst.at[:, g], go_recv.at[k]).start()

    def settle(k):
        arrived(stage.at[k], moved.at[k], k)
        for j in range(2):
            mine[k, j] = placed(j, lambda i: own[k, i], moved[k, 0], moved[k, 1])
        spread_planes(mine.at[k], cells.at[k], k)

    def wide(ref_value):
        return ref_value.astype(F32).reshape(ch, plane)

    move(0)

    def send_late(i, carry):
        peer = far_first(i)
        remote(own.at[pl.ds(late, 2), :, :, lanes_of(peer)], last.at[:, :, g], go_send.at[late], go_recv.at[late],
               (d, peer)).start()
        return carry

    lax.fori_loop(1, grps, send_late, 0)
    pltpu.make_async_copy(own.at[pl.ds(late, 2), :, :, lanes_of(g)], last.at[:, :, g], go_recv.at[late]).start()
    for k in range(1, late):
        loads[k].wait()
        move(k)
    for k in range(late):
        settle(k)

    r = lax.broadcasted_iota(jnp.int32, (plane, plane), 0)
    c = lax.broadcasted_iota(jnp.int32, (plane, plane), 1)
    ry, rz, cy, cz = r // side, r % side, c // side, c % side
    beside_cell = ((ry == cy) & (jnp.abs(rz - cz) == 1)) | ((rz == cz) & (jnp.abs(ry - cy) == 1))
    adj[...] = jnp.where(r == c, -6.0, jnp.where(beside_cell, 1.0, 0.0)).astype(BF16)
    width = 8 * side

    def layer_cell(layer, k):
        along_y = jnp.where(layer == 0, k, plane - side + k)
        along_z = jnp.where(layer == 2, k * side, k * side + side - 1)
        return jnp.where(layer < 2, along_y, along_z)

    r = lax.broadcasted_iota(jnp.int32, (plane, width), 0)
    c = lax.broadcasted_iota(jnp.int32, (plane, width), 1)
    for j in range(2):
        hit = (r == layer_cell((c // side) % 4, c % side)) & (c // (4 * side) == j)
        pick[j] = jnp.where(hit, 1.0, 0.0).astype(BF16)
    r = lax.broadcasted_iota(jnp.int32, (width, plane), 0)
    c = lax.broadcasted_iota(jnp.int32, (width, plane), 1)
    layer = (r // side) % 4
    opposite = jnp.where(layer % 2 == 0, layer + 1, layer - 1)
    place[...] = jnp.where(c == layer_cell(opposite, r % side), 1.0, 0.0).astype(BF16)
    bcol[...] = jnp.broadcast_to(bias[...], (bcol.shape[1], hid)).T
    wait_for(last, go_recv.at[late])
    for k in (hist_len - 1, late):
        r = k - late
        for to, which in enumerate((go_right, go_left)):
            stage_last[r, to] = jnp.where(which == 1, last[r, 1], last[r, 0])
        start_moves(stage_last.at[r], moved_last.at[r], k)
    loads[hist_len].wait()
    loads[hist_len + 1].wait()
    for k in range(hist_len + 1):
        wt[:, k * ch:(k + 1) * ch] = w_raw[k * ch:(k + 1) * ch, :].astype(F32).T.astype(BF16)
    wot[...] = wo_raw[...].astype(F32).T.astype(BF16)

    lane = lax.broadcasted_iota(jnp.int32, (ch, width), 1)
    lane_layer, lane_patch = (lane // side) % 4, lane // (4 * side)

    def halo_copies(t, state, xm, xp, j):
        sem = lambda i: (halo_send.at[t, 5 * j + i], halo_recv.at[t, 5 * j + i])
        return (remote(state.at[j], xm.at[2 + j], *sem(0), (d, up)),
                remote(state.at[j], xp.at[2 + j], *sem(1), (d, down)))

    def rim_copies(t, state, buf, j):
        sem = lambda i: (halo_send.at[t, 5 * j + i], halo_recv.at[t, 5 * j + i])
        return ((has_right, remote(state.at[j], buf.at[j], *sem(2), (right, 1 - g))),
                (has_left, remote(state.at[j], buf.at[4 + j], *sem(3), (left, 1 - g))))

    def edge_copies(t, edge):
        return ((has_right, remote(edge.at[1], edge.at[0], halo_send.at[t, 4], halo_recv.at[t, 4], (right, g))),
                (has_left, remote(edge.at[1], edge.at[2], halo_send.at[t, 9], halo_recv.at[t, 9], (left, g))))

    def start_halo(t, state, xm, xp, j):
        for at, buf in ((0, xm), (1, xp)):
            for there, copy in rim_copies(t, state, buf, j):
                pl.when((g == at) & there)(copy.start)
        for copy in halo_copies(t, state, xm, xp, j):
            copy.start()

    def start_edges(t, state, edge):
        edges = sum(jnp.dot(wide(state[j]).astype(BF16), pick[j], preferred_element_type=F32) for j in range(2))
        edge[1] = edges.astype(BF16)
        for there, copy in edge_copies(t, edge):
            pl.when(there)(copy.start)

    def finish_halo(t, state, xm, xp, edge):
        for j in range(2):
            for copy in halo_copies(t, state, xm, xp, j):
                copy.wait()
            for at, out_buf, in_buf in ((0, xm, xp), (1, xp, xm)):
                (_, to_right), (_, to_left) = rim_copies(t, state, out_buf, j)
                (_, from_left), (_, from_right) = rim_copies(t, state, in_buf, j)
                for there, copy in ((has_right, to_right), (has_left, to_left)):
                    pl.when((g == at) & there)(copy.wait_send)
                for there, copy in ((has_left, from_left), (has_right, from_right)):
                    pl.when((g == at) & there)(copy.wait_recv)
        (_, right_edge), (_, left_edge) = edge_copies(t, edge)
        pl.when(has_right)(right_edge.wait_send)
        pl.when(has_left)(left_edge.wait_send)
        pl.when(has_left)(right_edge.wait_recv)
        pl.when(has_right)(left_edge.wait_recv)

    def laplace(state, xm, xp, edge, j):
        near = jnp.dot(wide(state[j]).astype(BF16), adj[...], preferred_element_type=F32)
        slots = beside_slot[j]
        wanted = jnp.where(lane_layer == 0, slots[3], jnp.where(lane_layer == 1, slots[2], jnp.where(
            lane_layer == 2, slots[5], slots[4])))
        faces = jnp.zeros((ch, width), F32)
        for i in range(3):
            faces = jnp.where(wanted == 2 * i + lane_patch, edge[i].astype(F32), faces)
        near = near + jnp.dot(faces.astype(BF16), place[...], preferred_element_type=F32)
        before = xm[jnp.where(my_plane == 0, slots[0], 2 + j)]
        after = xp[jnp.where(my_plane == grps - 1, slots[1], 2 + j)]
        return (near + wide(before) + wide(after)).astype(BF16)

    def times(k, rows):
        return jnp.dot(wt[:, k * ch:(k + 1) * ch], rows, preferred_element_type=F32)

    cols = [slice(j * plane, (j + 1) * plane) for j in range(2)]

    def next_state(pre, start, j):
        hidden = (pre / (1.0 + jnp.exp(-pre))).astype(BF16)
        update = jnp.dot(wot[...], hidden, preferred_element_type=F32).astype(BF16)
        fresh = start + step_size[j] * update.astype(F32)
        return fresh.reshape(grps, block, plane).astype(BF16)

    def send_back(t, state):
        def send(i, carry):
            peer = far_first(i)
            remote(state.at[:, peer], out.at[:, t, :, lanes_of(g)], back_send.at[t], back_recv.at[t],
                   (d, peer)).start()
            return carry

        lax.fori_loop(1, grps, send, 0)
        pltpu.make_async_copy(state.at[:, g], out.at[:, t, :, lanes_of(g)], back_recv.at[t]).start()

    newest = cells.at[0]
    wait_for(newest, go_recv.at[0])
    for j in range(2):
        start_halo(0, newest, xm1, xp1, j)
    start_edges(0, newest, edge1)
    wide_bias = jnp.concatenate([bcol[...]] * (plane // bcol.shape[1]), 1)
    for j in range(2):
        rows = wide(newest[j]).astype(BF16)
        base1[:, cols[j]] = wide_bias + times(0, rows)
        base2[:, cols[j]] = wide_bias + times(1, rows)
    for k in (hist_len - 1, late):
        r = k - late
        arrived(stage_last.at[r], moved_last.at[r], k)
        for j in range(2):
            rows = placed(j, lambda i: last[r, i].astype(F32), moved_last[r, 0].astype(F32), moved_last[r, 1].astype(F32))
            rows = rows.reshape(ch, plane).astype(BF16)
            base1[:, cols[j]] += times(k, rows)
            if k + 1 < hist_len:
                base2[:, cols[j]] += times(k + 1, rows)
    finish_halo(0, newest, xm1, xp1, edge1)
    for j in range(2):
        base1[:, cols[j]] += times(hist_len, laplace(newest, xm1, xp1, edge1, j))
    for k in range(1, late):
        wait_for(cells.at[k], go_recv.at[k])
    for j in range(2):
        pre = base1[:, cols[j]]
        for k in range(1, late):
            pre = pre + times(k, wide(cells[k, j]).astype(BF16))
        state1[j] = next_state(pre, wide(newest[j]), j)
        start_halo(1, state1, xm2, xp2, j)
    start_edges(1, state1, edge2)
    send_back(0, state1)
    for j in range(2):
        more = times(0, wide(state1[j]).astype(BF16))
        for k in range(1, late):
            more = more + times(k + 1, wide(cells[k, j]).astype(BF16))
        base2[:, cols[j]] += more
    finish_halo(1, state1, xm2, xp2, edge2)
    for j in range(2):
        pre = base2[:, cols[j]] + times(hist_len, laplace(state1, xm2, xp2, edge2, j))
        state2[j] = next_state(pre, wide(state1[j]), j)
    send_back(1, state2)

    for k in range(hist_len):
        src, dst = (stage.at[k], moved.at[k]) if k < late else (stage_last.at[k - late], moved_last.at[k - late])
        for there, copy in sent(src, dst, k):
            pl.when(there)(copy.wait_send)
        if k < late:
            wait_for(last.at[0, :, pl.ds(0, grps - 1)], go_send.at[k])
    wait_for(last.at[:, :, pl.ds(0, grps - 1)], go_send.at[late])
    for t in range(2):
        wait_for(state1.at[:, pl.ds(0, grps - 1)], back_send.at[t])
        wait_for(out.at[:, t], back_recv.at[t])


def solution(mesh):
    doms, grps = mesh.shape["dom"], mesh.shape["grp"]

    def local(history, face_patch, refined, dest_slot, w_in, in_bias, w_out):
        per_dev, hist_len, block, cell_count = history.shape
        hid, ch = w_out.shape
        side = round(cell_count ** (1 / 3))
        plane = side * side
        width = 8 * side
        sizes = (doms, grps, side, hist_len, ch, hid)
        anywhere = pl.BlockSpec(memory_space=pl.ANY)
        vmem, dma = pltpu.VMEM, pltpu.SemaphoreType.DMA
        column = min(128, plane)
        states = pl.pallas_call(
            functools.partial(surrogate, sizes),
            out_shape=pltpu.VMEM((per_dev, 2, block, cell_count), BF16),
            in_specs=[anywhere] * 7,
            out_specs=pl.BlockSpec(memory_space=pltpu.VMEM),
            scratch_shapes=[
                pltpu.SMEM(dest_slot.shape, jnp.int32),
                pltpu.SMEM(face_patch.shape[::-1], jnp.int32),
                pltpu.SMEM(refined.shape, jnp.int32),
                vmem((1, hid), F32),
                vmem((hist_len, per_dev, block, cell_count), BF16),
                *[vmem((hist_len - 2, 2, block, cell_count), BF16) for _ in range(3)],
                vmem((hist_len - 2, per_dev, grps, block, plane), BF16),
                *[vmem((2, 2, grps, block, plane), BF16) for _ in range(3)],
                vmem((per_dev, grps, block, plane), BF16),
                vmem((per_dev, grps, block, plane), BF16),
                *[vmem((7, grps, block, plane), BF16) for _ in range(4)],
                *[vmem((3, ch, width), BF16) for _ in range(2)],
                vmem(w_in.shape, BF16),
                vmem(w_out.shape, BF16),
                vmem((hid, w_in.shape[0]), BF16),
                vmem((ch, hid), BF16),
                vmem((hid, column), F32),
                *[vmem((hid, per_dev * plane), F32) for _ in range(2)],
                vmem((plane, plane), BF16),
                vmem((2, plane, width), BF16),
                vmem((width, plane), BF16),
                dma((hist_len + 6,)),
                dma((hist_len, 2)),
                dma((hist_len, 2)),
                dma((hist_len,)),
                dma((hist_len,)),
                dma((2,)),
                dma((2,)),
                dma((2, 10)),
                dma((2, 10)),
            ],
            compiler_params=pltpu.CompilerParams(
                collective_id=0, has_side_effects=True, vmem_limit_bytes=60 * 2**20),
            name="surrogate",
        )(dest_slot, face_patch.T, refined, history, w_in, w_out, in_bias.reshape(1, hid))
        return states

    placed = (P("dom", None, "grp", None), P(), P(), P(), P(), P(), P())
    return jax.shard_map(
        local, mesh=mesh, in_specs=placed, out_specs=P("dom", None, "grp", None), check_vma=False
    )
```

```python
import functools

import jax
import jax.numpy as jnp
from jax import lax
from jax.experimental import pallas as pl
from jax.experimental.pallas import tpu as pltpu
from jax.sharding import PartitionSpec as P

MESH = pl.DeviceIdType.MESH
F32, BF16 = jnp.float32, jnp.bfloat16


def surrogate(sizes, dest_in, face_in, refined_in, hist, w_in, w_out, bias_in, out, dest, face, refined, bias, own, stage, moved, mine, cells, last, stage_last,
              moved_last, state1, state2, xm1, xp1, xm2, xp2, edge1, edge2, w_raw, wo_raw, wt, wot, bcol, base1, base2,
              adj, pick, place, load_sem, mig_send, mig_recv, go_send, go_recv, back_send, back_recv, halo_send,
              halo_recv):
    doms, grps, side, hist_len, ch, hid = sizes
    plane = side * side
    block = ch // grps
    late = hist_len - 2
    d, g = lax.axis_index("dom"), lax.axis_index("grp")
    left, right = d - 1, d + 1
    has_left, has_right = d > 0, d < doms - 1
    up, down = lax.rem(g + 1, grps), lax.rem(g + grps - 1, grps)
    my_plane = down

    def wait_for(ref, sem):
        pltpu.make_async_copy(ref, ref, sem).wait()

    def remote(src, dst, send_sem, recv_sem, to):
        return pltpu.make_async_remote_copy(
            src_ref=src, dst_ref=dst, send_sem=send_sem, recv_sem=recv_sem, device_id=to, device_id_type=MESH)

    loads = [pltpu.make_async_copy(hist.at[:, k], own.at[k], load_sem.at[k]) for k in range(hist_len)]
    loads.append(pltpu.make_async_copy(w_in, w_raw, load_sem.at[hist_len]))
    loads.append(pltpu.make_async_copy(w_out, wo_raw, load_sem.at[hist_len + 1]))
    small = ((dest_in, dest), (face_in, face), (refined_in, refined), (bias_in, bias))
    tables = [pltpu.make_async_copy(src, dst, load_sem.at[hist_len + 2 + i]) for i, (src, dst) in enumerate(small)]

    def far_first(i):
        half = lax.div(i, 2)
        return lax.rem(g + grps // 2 + jnp.where(lax.rem(i, 2) == 0, half, -half), grps)

    first = [loads[0]] + loads[late:hist_len]
    for load in first:
        load.start()

    barrier = pltpu.get_barrier_semaphore()

    def greet(i, carry):
        pl.semaphore_signal(barrier, inc=1, device_id=(d, far_first(i)), device_id_type=MESH)
        return carry

    lax.fori_loop(1, grps, greet, 0)
    for there, beside in ((has_left, left), (has_right, right)):
        @pl.when(there)
        def _(beside=beside):
            pl.semaphore_signal(barrier, inc=1, device_id=(beside, g), device_id_type=MESH)

            @pl.when(g < 2)
            def _():
                pl.semaphore_signal(barrier, inc=1, device_id=(beside, 1 - g), device_id_type=MESH)

    for load in tables + loads[1:late] + loads[hist_len:]:
        load.start()
    for table in tables:
        table.wait()

    patches = 2 * doms
    cands = [lax.rem(2 * d + patches - 2 + i, patches) for i in range(6)]
    goals = [dest[c] for c in cands]
    go_left = jnp.where(goals[3] // 2 == d - 1, 1, 0)
    go_right = jnp.where(goals[3] // 2 == d + 1, 1, 0)
    origin, beside_slot, step_size = [], [], []
    for j in range(2):
        place_of = jnp.int32(0)
        owner = jnp.int32(0)
        for i in range(6):
            hit = goals[i] == 2 * d + j
            place_of = jnp.where(hit, i, place_of)
            owner = jnp.where(hit, cands[i], owner)
        origin.append(place_of)
        row = []
        for f in range(6):
            q = face[f, owner]
            pos = jnp.clip(dest[jnp.maximum(q, 0)] - 2 * (d - 1), 0, 5)
            row.append(jnp.where(q >= 0, pos, 6))
        beside_slot.append(row)
        step_size.append(1.0 - 0.5 * refined[owner].astype(F32))

    def placed(j, mine_of, from_left, from_right):
        at = origin[j]
        stays = jnp.where(at == 2, mine_of(0), mine_of(1))
        comes = jnp.where(at < 2, from_left, from_right)
        return jnp.where((at == 2) | (at == 3), stays, comes)

    for buf in (xm1, xp1, xm2, xp2):
        buf[6] = jnp.zeros(buf.shape[1:], BF16)
    for load in first:
        load.wait()
    beside_count = jnp.where(has_left, 1, 0) + jnp.where(has_right, 1, 0)
    pl.semaphore_wait(barrier, grps - 1 + beside_count * jnp.where(g < 2, 2, 1))

    def sent(src, dst, k):
        return [(has_right, remote(src.at[0], dst.at[0], mig_send.at[k, 0], mig_recv.at[k, 0], (right, g))),
                (has_left, remote(src.at[1], dst.at[1], mig_send.at[k, 1], mig_recv.at[k, 1], (left, g)))]

    def move(k):
        for to, which in enumerate((go_right, go_left)):
            stage[k, to] = jnp.where(which == 1, own[k, 1], own[k, 0])
        start_moves(stage.at[k], moved.at[k], k)

    def start_moves(src, dst, k):
        for there, copy in sent(src, dst, k):
            pl.when(there)(copy.start)

    def arrived(src, dst, k):
        (_, from_left), (_, from_right) = sent(src, dst, k)
        pl.when(has_left)(from_left.wait_recv)
        pl.when(has_right)(from_right.wait_recv)

    def lanes_of(device):
        return pl.ds(pl.multiple_of(lax.rem(device + grps - 1, grps) * plane, plane), plane)

    def spread_planes(src, dst, k):
        def send(i, carry):
            peer = far_first(i)
            remote(src.at[:, :, lanes_of(peer)], dst.at[:, g], go_send.at[k], go_recv.at[k], (d, peer)).start()
            return carry

        lax.fori_loop(1, grps, send, 0)
        pltpu.make_async_copy(src.at[:, :, lanes_of(g)], dst.at[:, g], go_recv.at[k]).start()

    def settle(k):
        arrived(stage.at[k], moved.at[k], k)
        for j in range(2):
            mine[k, j] = placed(j, lambda i: own[k, i], moved[k, 0], moved[k, 1])
        spread_planes(mine.at[k], cells.at[k], k)

    def wide(ref_value):
        return ref_value.astype(F32).reshape(ch, plane)

    def send_late(i, carry):
        peer = far_first(i)
        remote(own.at[pl.ds(late, 2), :, :, lanes_of(peer)], last.at[:, :, g], go_send.at[late], go_recv.at[late],
               (d, peer)).start()
        return carry

    lax.fori_loop(1, grps, send_late, 0)
    pltpu.make_async_copy(own.at[pl.ds(late, 2), :, :, lanes_of(g)], last.at[:, :, g], go_recv.at[late]).start()
    move(0)
    for k in range(1, late):
        loads[k].wait()
        move(k)
    for k in range(late):
        settle(k)

    r = lax.broadcasted_iota(jnp.int32, (plane, plane), 0)
    c = lax.broadcasted_iota(jnp.int32, (plane, plane), 1)
    ry, rz, cy, cz = r // side, r % side, c // side, c % side
    beside_cell = ((ry == cy) & (jnp.abs(rz - cz) == 1)) | ((rz == cz) & (jnp.abs(ry - cy) == 1))
    adj[...] = jnp.where(r == c, -6.0, jnp.where(beside_cell, 1.0, 0.0)).astype(BF16)
    width = 8 * side

    def layer_cell(layer, k):
        along_y = jnp.where(layer == 0, k, plane - side + k)
        along_z = jnp.where(layer == 2, k * side, k * side + side - 1)
        return jnp.where(layer < 2, along_y, along_z)

    r = lax.broadcasted_iota(jnp.int32, (plane, width), 0)
    c = lax.broadcasted_iota(jnp.int32, (plane, width), 1)
    for j in range(2):
        hit = (r == layer_cell((c // side) % 4, c % side)) & (c // (4 * side) == j)
        pick[j] = jnp.where(hit, 1.0, 0.0).astype(BF16)
    r = lax.broadcasted_iota(jnp.int32, (width, plane), 0)
    c = lax.broadcasted_iota(jnp.int32, (width, plane), 1)
    layer = (r // side) % 4
    opposite = jnp.where(layer % 2 == 0, layer + 1, layer - 1)
    place[...] = jnp.where(c == layer_cell(opposite, r % side), 1.0, 0.0).astype(BF16)
    bcol[...] = jnp.broadcast_to(bias[...], (bcol.shape[1], hid)).T
    wait_for(last, go_recv.at[late])
    for k in (hist_len - 1, late):
        r = k - late
        for to, which in enumerate((go_right, go_left)):
            stage_last[r, to] = jnp.where(which == 1, last[r, 1], last[r, 0])
        start_moves(stage_last.at[r], moved_last.at[r], k)
    loads[hist_len].wait()
    loads[hist_len + 1].wait()
    for k in range(hist_len + 1):
        wt[:, k * ch:(k + 1) * ch] = w_raw[k * ch:(k + 1) * ch, :].astype(F32).T.astype(BF16)
    wot[...] = wo_raw[...].astype(F32).T.astype(BF16)

    lane = lax.broadcasted_iota(jnp.int32, (ch, width), 1)
    lane_layer, lane_patch = (lane // side) % 4, lane // (4 * side)

    def halo_copies(t, state, xm, xp, j):
        sem = lambda i: (halo_send.at[t, 5 * j + i], halo_recv.at[t, 5 * j + i])
        return (remote(state.at[j], xm.at[2 + j], *sem(0), (d, up)),
                remote(state.at[j], xp.at[2 + j], *sem(1), (d, down)))

    def rim_copies(t, state, buf, j):
        sem = lambda i: (halo_send.at[t, 5 * j + i], halo_recv.at[t, 5 * j + i])
        return ((has_right, remote(state.at[j], buf.at[j], *sem(2), (right, 1 - g))),
                (has_left, remote(state.at[j], buf.at[4 + j], *sem(3), (left, 1 - g))))

    def edge_copies(t, edge):
        return ((has_right, remote(edge.at[1], edge.at[0], halo_send.at[t, 4], halo_recv.at[t, 4], (right, g))),
                (has_left, remote(edge.at[1], edge.at[2], halo_send.at[t, 9], halo_recv.at[t, 9], (left, g))))

    def start_halo(t, state, xm, xp, j):
        for at, buf in ((0, xm), (1, xp)):
            for there, copy in rim_copies(t, state, buf, j):
                pl.when((g == at) & there)(copy.start)
        for copy in halo_copies(t, state, xm, xp, j):
            copy.start()

    def start_edges(t, state, edge):
        edges = sum(jnp.dot(wide(state[j]).astype(BF16), pick[j], preferred_element_type=F32) for j in range(2))
        edge[1] = edges.astype(BF16)
        for there, copy in edge_copies(t, edge):
            pl.when(there)(copy.start)

    def finish_halo(t, state, xm, xp, edge):
        for j in range(2):
            for copy in halo_copies(t, state, xm, xp, j):
                copy.wait()
            for at, out_buf, in_buf in ((0, xm, xp), (1, xp, xm)):
                (_, to_right), (_, to_left) = rim_copies(t, state, out_buf, j)
                (_, from_left), (_, from_right) = rim_copies(t, state, in_buf, j)
                for there, copy in ((has_right, to_right), (has_left, to_left)):
                    pl.when((g == at) & there)(copy.wait_send)
                for there, copy in ((has_left, from_left), (has_right, from_right)):
                    pl.when((g == at) & there)(copy.wait_recv)
        (_, right_edge), (_, left_edge) = edge_copies(t, edge)
        pl.when(has_right)(right_edge.wait_send)
        pl.when(has_left)(left_edge.wait_send)
        pl.when(has_left)(right_edge.wait_recv)
        pl.when(has_right)(left_edge.wait_recv)

    def laplace(state, xm, xp, edge, j):
        near = jnp.dot(wide(state[j]).astype(BF16), adj[...], preferred_element_type=F32)
        slots = beside_slot[j]
        wanted = jnp.where(lane_layer == 0, slots[3], jnp.where(lane_layer == 1, slots[2], jnp.where(
            lane_layer == 2, slots[5], slots[4])))
        faces = jnp.zeros((ch, width), F32)
        for i in range(3):
            faces = jnp.where(wanted == 2 * i + lane_patch, edge[i].astype(F32), faces)
        near = near + jnp.dot(faces.astype(BF16), place[...], preferred_element_type=F32)
        before = xm[jnp.where(my_plane == 0, slots[0], 2 + j)]
        after = xp[jnp.where(my_plane == grps - 1, slots[1], 2 + j)]
        return (near + wide(before) + wide(after)).astype(BF16)

    def times(k, rows):
        return jnp.dot(wt[:, k * ch:(k + 1) * ch], rows, preferred_element_type=F32)

    cols = [slice(j * plane, (j + 1) * plane) for j in range(2)]

    def next_state(pre, start, j):
        hidden = (pre / (1.0 + jnp.exp(-pre))).astype(BF16)
        update = jnp.dot(wot[...], hidden, preferred_element_type=F32).astype(BF16)
        fresh = start + step_size[j] * update.astype(F32)
        return fresh.reshape(grps, block, plane).astype(BF16)

    def send_back(t, state):
        def send(i, carry):
            peer = far_first(i)
            remote(state.at[:, peer], out.at[:, t, :, lanes_of(g)], back_send.at[t], back_recv.at[t],
                   (d, peer)).start()
            return carry

        lax.fori_loop(1, grps, send, 0)
        pltpu.make_async_copy(state.at[:, g], out.at[:, t, :, lanes_of(g)], back_recv.at[t]).start()

    newest = cells.at[0]
    wait_for(newest, go_recv.at[0])
    for j in range(2):
        start_halo(0, newest, xm1, xp1, j)
    start_edges(0, newest, edge1)
    wide_bias = jnp.concatenate([bcol[...]] * (plane // bcol.shape[1]), 1)
    for j in range(2):
        rows = wide(newest[j]).astype(BF16)
        base1[:, cols[j]] = wide_bias + times(0, rows)
        base2[:, cols[j]] = wide_bias + times(1, rows)
    for k in (hist_len - 1, late):
        r = k - late
        arrived(stage_last.at[r], moved_last.at[r], k)
        for j in range(2):
            rows = placed(j, lambda i: last[r, i].astype(F32), moved_last[r, 0].astype(F32), moved_last[r, 1].astype(F32))
            rows = rows.reshape(ch, plane).astype(BF16)
            base1[:, cols[j]] += times(k, rows)
            if k + 1 < hist_len:
                base2[:, cols[j]] += times(k + 1, rows)
    finish_halo(0, newest, xm1, xp1, edge1)
    for j in range(2):
        base1[:, cols[j]] += times(hist_len, laplace(newest, xm1, xp1, edge1, j))
    for k in range(1, late):
        wait_for(cells.at[k], go_recv.at[k])
    for j in range(2):
        pre = base1[:, cols[j]]
        for k in range(1, late):
            pre = pre + times(k, wide(cells[k, j]).astype(BF16))
        state1[j] = next_state(pre, wide(newest[j]), j)
        start_halo(1, state1, xm2, xp2, j)
    start_edges(1, state1, edge2)
    send_back(0, state1)
    for j in range(2):
        more = times(0, wide(state1[j]).astype(BF16))
        for k in range(1, late):
            more = more + times(k + 1, wide(cells[k, j]).astype(BF16))
        base2[:, cols[j]] += more
    finish_halo(1, state1, xm2, xp2, edge2)
    for j in range(2):
        pre = base2[:, cols[j]] + times(hist_len, laplace(state1, xm2, xp2, edge2, j))
        state2[j] = next_state(pre, wide(state1[j]), j)
    send_back(1, state2)

    for k in range(hist_len):
        src, dst = (stage.at[k], moved.at[k]) if k < late else (stage_last.at[k - late], moved_last.at[k - late])
        for there, copy in sent(src, dst, k):
            pl.when(there)(copy.wait_send)
        if k < late:
            wait_for(last.at[0, :, pl.ds(0, grps - 1)], go_send.at[k])
    wait_for(last.at[:, :, pl.ds(0, grps - 1)], go_send.at[late])
    for t in range(2):
        wait_for(state1.at[:, pl.ds(0, grps - 1)], back_send.at[t])
        wait_for(out.at[:, t], back_recv.at[t])


def solution(mesh):
    doms, grps = mesh.shape["dom"], mesh.shape["grp"]

    def local(history, face_patch, refined, dest_slot, w_in, in_bias, w_out):
        per_dev, hist_len, block, cell_count = history.shape
        hid, ch = w_out.shape
        side = round(cell_count ** (1 / 3))
        plane = side * side
        width = 8 * side
        sizes = (doms, grps, side, hist_len, ch, hid)
        anywhere = pl.BlockSpec(memory_space=pl.ANY)
        vmem, dma = pltpu.VMEM, pltpu.SemaphoreType.DMA
        column = min(128, plane)
        states = pl.pallas_call(
            functools.partial(surrogate, sizes),
            out_shape=pltpu.VMEM((per_dev, 2, block, cell_count), BF16),
            in_specs=[anywhere] * 7,
            out_specs=pl.BlockSpec(memory_space=pltpu.VMEM),
            scratch_shapes=[
                pltpu.SMEM(dest_slot.shape, jnp.int32),
                pltpu.SMEM(face_patch.shape[::-1], jnp.int32),
                pltpu.SMEM(refined.shape, jnp.int32),
                vmem((1, hid), F32),
                vmem((hist_len, per_dev, block, cell_count), BF16),
                *[vmem((hist_len - 2, 2, block, cell_count), BF16) for _ in range(3)],
                vmem((hist_len - 2, per_dev, grps, block, plane), BF16),
                *[vmem((2, 2, grps, block, plane), BF16) for _ in range(3)],
                vmem((per_dev, grps, block, plane), BF16),
                vmem((per_dev, grps, block, plane), BF16),
                *[vmem((7, grps, block, plane), BF16) for _ in range(4)],
                *[vmem((3, ch, width), BF16) for _ in range(2)],
                vmem(w_in.shape, BF16),
                vmem(w_out.shape, BF16),
                vmem((hid, w_in.shape[0]), BF16),
                vmem((ch, hid), BF16),
                vmem((hid, column), F32),
                *[vmem((hid, per_dev * plane), F32) for _ in range(2)],
                vmem((plane, plane), BF16),
                vmem((2, plane, width), BF16),
                vmem((width, plane), BF16),
                dma((hist_len + 6,)),
                dma((hist_len, 2)),
                dma((hist_len, 2)),
                dma((hist_len,)),
                dma((hist_len,)),
                dma((2,)),
                dma((2,)),
                dma((2, 10)),
                dma((2, 10)),
            ],
            compiler_params=pltpu.CompilerParams(
                collective_id=0, has_side_effects=True, vmem_limit_bytes=60 * 2**20),
            name="surrogate",
        )(dest_slot, face_patch.T, refined, history, w_in, w_out, in_bias.reshape(1, hid))
        return states

    placed = (P("dom", None, "grp", None), P(), P(), P(), P(), P(), P())
    return jax.shard_map(
        local, mesh=mesh, in_specs=placed, out_specs=P("dom", None, "grp", None), check_vma=False
    )
```
